32 devices in a mesh: grp: 4 (over z), rd: 8 (over y, x, core).
Axes of the slice: x: 2, y: 2, z: 4, core: 2. Of those that a mesh axis runs over, the one named last changes fastest.
Arguments:
- label_scores: bfloat16 [32768, 512], P(('grp', 'rd')), may hold values from -6 to 6
- degree: float32 [32768], P(('grp', 'rd')), may hold values from 1 to 4
- seed_label: int32 [8192], P(('grp', 'rd')), may hold values from 0 to 1023
- wanted: int32 [4, 8, 8, 2], P('grp', 'rd'), may hold values from -1 to 3, as said below
- nbr_slot: int32 [4, 8, 4, 24], P('grp', 'rd'), may hold values from 0 to 15, as said below
- tiles: bfloat16 [4, 8, 4, 24, 256, 256], P('grp', 'rd'), may hold values from 0 to 0.025512695
Outputs:
- new_scores: float32 [8192, 512], P(('grp', 'rd'))
The draws below stay inside these ranges and needn't reach their ends.
Inputs may be any that keep to these rules, and one draw needn't show every extreme that they name: `wanted`: for each reader and each device of its column group, the live slots come first and hold distinct block indices of that device; each reader takes one or more blocks from every device of its group and exactly 2 from some device; -1 marks an empty slot. `nbr_slot`: each entry is the number s * 2 + c of a live slot of the same column group and reader in wanted; every live slot is named at least once.
All inputs are finite; a program needn't handle non-finite values.
Results may differ from the reference program's by a relative error of at most 0.0029.
Values may be sent and summed in bfloat16 or wider, within the bound.
A program may use at most 192 MiB of HBM per device.

```python
import math
import jax
import jax.numpy as jnp
from jax import lax

BLOCK = 256
CLASSES = 512
K = 24
CAP = 2
OWN = 4
ROWS = 32768
OUT_ROWS = 8192
N_GRP = 4
N_RD = 8


def plan_tables(key):
    key = jax.random.fold_in(key, 11)
    key_count, key_full, key_local, key_extra, key_mix = jax.random.split(key, 5)
    slot_total = N_RD * CAP
    entries = N_GRP * K
    counts = jax.random.randint(key_count, (N_GRP, N_RD, N_RD), 1, CAP + 1)
    full_at = jax.random.randint(key_full, (N_GRP, N_RD), 0, N_RD)
    counts = jnp.where(jnp.arange(N_RD)[None, None, :] == full_at[:, :, None], CAP, counts)
    scores = jax.random.randint(key_local, (N_GRP, N_RD, N_RD, OWN), 0, 1 << 20) * OWN + jnp.arange(OWN)
    chosen = jnp.argsort(scores, axis=-1, stable=True)[..., :CAP]
    live_slot = jnp.arange(CAP)[None, None, None, :] < counts[..., None]
    wanted_table = jnp.where(live_slot, chosen, -1).astype(jnp.int32)
    live_flat = live_slot.reshape(N_GRP, N_RD, slot_total)
    live_order = jnp.argsort(jnp.where(live_flat, 0, 1) * slot_total + jnp.arange(slot_total), axis=-1, stable=True)
    live_total = jnp.sum(live_flat.astype(jnp.int32), axis=-1)
    extra_pick = jax.random.randint(key_extra, (N_GRP, N_RD, entries), 0, live_total[..., None])
    position = jnp.arange(entries)[None, None, :]
    picks = jnp.where(position < live_total[..., None], position, extra_pick)
    listed = jnp.take_along_axis(live_order, picks, axis=-1)
    mixing = jax.random.randint(key_mix, (N_GRP, N_RD, entries), 0, 1 << 20) * entries + position
    shuffle = jnp.argsort(mixing, axis=-1, stable=True)
    listed = jnp.take_along_axis(listed, shuffle, axis=-1)
    return (wanted_table, listed.reshape(N_GRP, N_RD, N_GRP, K).astype(jnp.int32))


def draw_wanted(key, part):
    return plan_tables(key)[0]


def draw_nbr_slot(key, part):
    return plan_tables(key)[1]


def with_ends(array, key, low, top_value):
    place = [jax.random.randint(jax.random.fold_in(key, axis), (), 0, length) for axis, length in enumerate(array.shape)]
    main_axis = array.shape.index(max(array.shape))
    next_to = place[:main_axis] + [(place[main_axis] + 1) % array.shape[main_axis]] + place[main_axis + 1:]
    return array.at[tuple(place)].set(low).at[tuple(next_to)].set(top_value)


def steps_of(stream_key, shape, cuts, low, high):
    def one(dim, blocks):
        heights = jax.random.uniform(jax.random.fold_in(jax.random.fold_in(stream_key, 6), dim), (blocks,), jnp.float32, low / len(cuts), high / len(cuts))
        return jnp.repeat(jnp.exp(heights), shape[dim] // blocks).reshape((-1,) + (1,) * (len(shape) - dim - 1))

    level = one(*cuts[0])
    for cut in cuts[1:]:
        level = level * one(*cut)
    return level


def bell_draw(stream_key, shape, width, limit, pieces=(), kind=jnp.bfloat16):
    result = width * jax.random.normal(stream_key, shape, jnp.float32)
    if pieces:
        result = result * steps_of(stream_key, shape, pieces, -0.22, 0.18)
    return jnp.clip(result, -limit, limit).astype(kind)


def setup_inputs(seed: int = 0) -> dict:
    streams_of = jax.random.split(jax.random.key(seed), 7)
    label_scores = bell_draw(streams_of[0], (ROWS, CLASSES), 1.0, 6.0, ((0, 32),))
    degree = jnp.clip(jnp.exp(math.log(4.0) - 1.3862944 * jax.random.uniform(streams_of[1], (ROWS,), jnp.float32) ** steps_of(streams_of[1], (ROWS,), ((0, 32),), -0.2, 0.2)), 1.0, 4.0)
    seed_label = with_ends(jax.random.randint(streams_of[2], (OUT_ROWS,), 0, 2 * CLASSES), jax.random.fold_in(streams_of[2], 1), 0, (2 * CLASSES) - 1).astype(jnp.int32)
    wanted = draw_wanted(jax.random.fold_in(streams_of[6], 71), 0)
    nbr_slot = draw_nbr_slot(jax.random.fold_in(streams_of[6], 71), 0)
    tiles = jnp.clip(0.025512695 * jax.random.uniform(streams_of[5], (N_GRP, N_RD, N_GRP, K, BLOCK, BLOCK), jnp.float32) ** steps_of(streams_of[5], (N_GRP, N_RD, N_GRP, K, BLOCK, BLOCK), ((0, 4), (1, 8)), -0.2, 0.2), 0.0, 0.025512695).astype(jnp.bfloat16)
    return dict(label_scores=label_scores, degree=degree, seed_label=seed_label, wanted=wanted, nbr_slot=nbr_slot, tiles=tiles)


def reference(label_scores, degree, seed_label, wanted, nbr_slot, tiles):
    scaled = (label_scores * lax.rsqrt(degree)[:, None]).astype(jnp.bfloat16)
    scaled = scaled.reshape(N_GRP, N_RD * OWN, BLOCK, CLASSES)
    group_ids = (jnp.arange(N_GRP * N_RD) // N_RD).astype(jnp.int32)
    wanted_flat = wanted.reshape(N_GRP * N_RD, N_RD, CAP)
    slots_flat = nbr_slot.reshape(N_GRP * N_RD, N_GRP * K)
    tiles_flat = tiles.reshape(N_GRP * N_RD, N_GRP, K, BLOCK, BLOCK)

    def one_reader(packed):
        group_id, wanted_one, slots_one, tiles_one = packed
        source_block = jnp.arange(N_RD, dtype=jnp.int32)[:, None] * OWN + jnp.maximum(wanted_one, 0)
        block_index = source_block.reshape(-1)[slots_one].astype(jnp.int32)
        group_rows = scaled[group_id]
        fetched = group_rows[block_index].astype(jnp.float32).reshape(N_GRP, K, BLOCK, CLASSES)
        return jnp.einsum('qkij,qkjc->qic', tiles_one.astype(jnp.float32), fetched, precision=lax.Precision.HIGHEST)
    partials = lax.map(one_reader, (group_ids, wanted_flat, slots_flat, tiles_flat))
    summed = lax.optimization_barrier(jnp.sum(partials.reshape(N_GRP, N_RD, N_GRP, BLOCK, CLASSES), axis=0))
    spread = jnp.transpose(summed, (1, 0, 2, 3)).reshape(N_GRP * N_RD * BLOCK, CLASSES)
    degree_out = degree.reshape(N_GRP * N_RD, OWN * BLOCK)[:, :BLOCK].reshape(-1)
    onehot = (seed_label[:, None] == jnp.arange(CLASSES, dtype=jnp.int32)[None, :]).astype(jnp.float32)
    return 0.8 * lax.rsqrt(degree_out)[:, None] * spread + 0.2 * onehot
```

```python
import functools
import math

import jax
import jax.numpy as jnp
from jax import lax
from jax.experimental import pallas as pl
from jax.experimental.pallas import tpu as pltpu
from jax.sharding import PartitionSpec as P

MESH_ID = pl.DeviceIdType.MESH
CHUNK = 128
UNROLL = 8


def spread_kernel(
    dims, labels, degree, wanted, slots, tiles_hbm, out, *scratch
):
    groups, y_size, x_size, own, rows, near, chunks, cap = dims
    pool = scratch[:chunks]
    sent = scratch[chunks : 2 * chunks]
    landed = scratch[2 * chunks : 3 * chunks]
    tiles, tile_sem, x_send, x_recv, y_send, y_recv, s_send, s_recv, z_send, z_recv = scratch[
        3 * chunks :
    ]
    g = lax.axis_index("grp")
    me = lax.axis_index("rd")
    core = lax.rem(me, 2)
    x = lax.rem(lax.div(me, 2), x_size)
    y = lax.div(me, 2 * x_size)
    half = own // 2

    def device(yy, xx, cc):
        return (yy * x_size + xx) * 2 + cc

    def x_at(step):
        return lax.rem(x + step, x_size)

    def y_at(step):
        return lax.rem(y + step, y_size)

    sibling = device(y, x, 1 - core)

    tile_copies = []
    for d in range(groups):
        q = lax.rem(g + d, groups)
        copy = pltpu.make_async_copy(
            tiles_hbm.at[0, 0, q], tiles.at[pl.ds(q * near, near)], tile_sem.at[d]
        )
        tile_copies.append(copy)

    barrier = pltpu.get_barrier_semaphore()
    peers = [(g, device(y, x_at(i), core)) for i in range(1, x_size)]
    peers += [(g, device(y_at(i), x, core)) for i in range(1, y_size)]
    peers += [(g, sibling)]
    peers += [(lax.rem(g + d, groups), me) for d in range(1, groups)]
    for peer in peers:
        pl.semaphore_signal(barrier, inc=1, device_id=peer, device_id_type=MESH_ID)
    for copy in tile_copies:
        copy.start()

    lanes = 128
    eye = lax.broadcasted_iota(jnp.int32, (lanes, lanes), 0) == lax.broadcasted_iota(
        jnp.int32, (lanes, lanes), 1
    )

    def scale(part, carry):
        row = degree[pl.ds(part, 1), :]
        column = jnp.sum(
            jnp.where(eye, jnp.broadcast_to(row, (lanes, lanes)), 0.0), axis=1, keepdims=True
        )
        factor = lax.rsqrt(column)
        per_block = rows // lanes
        block = me * own + lax.div(part, per_block)
        first = lax.rem(part, per_block) * lanes
        for c in range(chunks):
            piece = labels[pl.ds(part * lanes, lanes), c * CHUNK : (c + 1) * CHUNK]
            pool[c][block, pl.ds(first, lanes), :] = (
                piece.astype(jnp.float32) * factor
            ).astype(jnp.bfloat16)
        return carry

    lax.fori_loop(0, own * rows // lanes, scale, 0)
    pl.semaphore_wait(barrier, len(peers))

    pending = []

    def copy_of(c, first, count, send, recv, target):
        view = pool[c].at[pl.ds(first, count)]
        return pltpu.make_async_remote_copy(
            src_ref=view,
            dst_ref=view,
            send_sem=send,
            recv_sem=recv,
            device_id=target,
            device_id_type=MESH_ID,
        )

    def x_copy(c, i, j, which, source, target):
        return copy_of(
            c,
            source * own + which * half,
            half,
            x_send.at[c, i, j, which],
            x_recv.at[c, i, j, which],
            (g, target),
        )

    def y_copy(c, i, j, which, source, target):
        return copy_of(
            c,
            source * own + which * half,
            half,
            y_send.at[c, i, j, which],
            y_recv.at[c, i, j, which],
            (g, target),
        )

    def s_copy(c, i, j, source):
        return copy_of(
            c, source * own, own, s_send.at[c, i, j], s_recv.at[c, i, j], (g, sibling)
        )

    def start(copy):
        copy.start()
        pending.append(copy)

    def send_own(c):
        for which in (0, 1):
            for j in range(1, x_size):
                start(x_copy(c, 0, j, which, me, device(y, x_at(j), core)))
            for i in range(1, y_size):
                start(y_copy(c, i, 0, 1 - which, me, device(y_at(i), x, core)))
        start(s_copy(c, 0, 0, me))

    def forward(c):
        for j in range(1, x_size):
            source = device(y, x_at(x_size - j), core)
            x_copy(c, 0, j, 0, source, sibling).wait_recv()
            for i in range(1, y_size):
                start(y_copy(c, i, j, 0, source, device(y_at(i), x, core)))
        for i in range(1, y_size):
            source = device(y_at(y_size - i), x, core)
            y_copy(c, i, 0, 1, source, sibling).wait_recv()
            for j in range(1, x_size):
                start(x_copy(c, i, j, 1, source, device(y, x_at(j), core)))

    def complete(c):
        for j in range(1, x_size):
            source = device(y, x_at(x_size - j), core)
            x_copy(c, 0, j, 1, source, sibling).wait_recv()
            start(s_copy(c, 0, j, source))
        for i in range(1, y_size):
            source = device(y_at(y_size - i), x, core)
            y_copy(c, i, 0, 0, source, sibling).wait_recv()
            start(s_copy(c, i, 0, source))
        for i in range(1, y_size):
            for j in range(1, x_size):
                source = device(y_at(y_size - i), x_at(x_size - j), core)
                y_copy(c, i, j, 0, source, sibling).wait_recv()
                x_copy(c, i, j, 1, source, sibling).wait_recv()
                start(s_copy(c, i, j, source))
        for i in range(y_size):
            for j in range(x_size):
                source = device(y_at(y_size - i), x_at(x_size - j), 1 - core)
                s_copy(c, i, j, source).wait_recv()

    def block_of(q, k):
        slot = slots[0, 0, q, k]
        source = lax.div(slot, cap)
        local = wanted[0, 0, source, lax.rem(slot, cap)]
        return source * own + jnp.maximum(local, 0)

    def z_copy(c, d):
        return pltpu.make_async_remote_copy(
            src_ref=sent[c].at[d - 1],
            dst_ref=landed[c].at[d - 1],
            send_sem=z_send.at[c, d - 1],
            recv_sem=z_recv.at[c, d - 1],
            device_id=(lax.rem(g + d, groups), me),
            device_id_type=MESH_ID,
        )

    order = sorted(range(1, groups), key=lambda d: abs(d - groups / 2)) + [0]

    def compute(c):
        for d in order:
            if c == 0:
                tile_copies[d].wait()
            q = lax.rem(g + d, groups)

            def body(step, acc):
                ks = [step * UNROLL + u for u in range(UNROLL)]
                left = jnp.concatenate([tiles[q * near + k] for k in ks], axis=1)
                right = jnp.concatenate([pool[c][block_of(q, k)] for k in ks], axis=0)
                return acc + jnp.dot(left, right, preferred_element_type=jnp.float32)

            acc = lax.fori_loop(
                0, near // UNROLL, body, jnp.zeros((rows, CHUNK), jnp.float32)
            )
            if d == 0:
                out[:, c * CHUNK : (c + 1) * CHUNK] = acc
            else:
                sent[c][d - 1] = acc.astype(jnp.bfloat16)
                start(z_copy(c, d))

    def finish(c):
        total = out[:, c * CHUNK : (c + 1) * CHUNK]
        for d in order[:-1]:
            z_copy(c, d).wait_recv()
            total = total + landed[c][d - 1].astype(jnp.float32)
        out[:, c * CHUNK : (c + 1) * CHUNK] = total

    send_own(0)
    if chunks > 1:
        send_own(1)
    forward(0)
    for c in range(chunks):
        if c + 2 < chunks:
            send_own(c + 2)
        if c + 1 < chunks:
            forward(c + 1)
        complete(c)
        compute(c)
    for c in range(chunks):
        finish(c)
    for copy in pending:
        copy.wait_send()


def per_device(groups, readers, label_scores, degree, seed_label, wanted, nbr_slot, tiles):
    rows = tiles.shape[-1]
    classes = label_scores.shape[1]
    own = label_scores.shape[0] // rows
    near = nbr_slot.shape[-1]
    cap = wanted.shape[-1]
    chunks = classes // CHUNK
    chips = readers // 2
    x_size = math.isqrt(chips)
    y_size = chips // x_size
    dims = (groups, y_size, x_size, own, rows, near, chunks, cap)
    dma = pltpu.SemaphoreType.DMA
    vmem = pl.BlockSpec(memory_space=pltpu.VMEM)
    smem = pl.BlockSpec(memory_space=pltpu.SMEM)
    spread = pl.pallas_call(
        functools.partial(spread_kernel, dims),
        out_shape=jax.ShapeDtypeStruct((rows, classes), jnp.float32),
        in_specs=[vmem, vmem, smem, smem, pl.BlockSpec(memory_space=pl.ANY)],
        out_specs=vmem,
        scratch_shapes=[
            pltpu.VMEM((readers * own, rows, CHUNK), jnp.bfloat16) for _ in range(chunks)
        ]
        + [pltpu.VMEM((groups - 1, rows, CHUNK), jnp.bfloat16) for _ in range(2 * chunks)]
        + [
            pltpu.VMEM((groups * near, rows, rows), jnp.bfloat16),
            dma((groups,)),
            dma((chunks, y_size, x_size, 2)),
            dma((chunks, y_size, x_size, 2)),
            dma((chunks, y_size, x_size, 2)),
            dma((chunks, y_size, x_size, 2)),
            dma((chunks, y_size, x_size)),
            dma((chunks, y_size, x_size)),
            dma((chunks, groups - 1)),
            dma((chunks, groups - 1)),
        ],
        compiler_params=pltpu.CompilerParams(
            collective_id=0, has_side_effects=True, vmem_limit_bytes=60 * 1024 * 1024
        ),
    )(label_scores, degree.reshape(-1, 128), wanted, nbr_slot, tiles)
    degree_out = degree[:rows]
    onehot = (seed_label[:, None] == jnp.arange(classes, dtype=jnp.int32)[None, :]).astype(
        jnp.float32
    )
    return 0.8 * lax.rsqrt(degree_out)[:, None] * spread + 0.2 * onehot


def solution(mesh):
    in_specs = (
        P(("grp", "rd"), None),
        P(("grp", "rd")),
        P(("grp", "rd")),
        P("grp", "rd", None, None),
        P("grp", "rd", None, None),
        P("grp", "rd", None, None, None, None),
    )
    out_specs = P(("grp", "rd"), None)
    body = functools.partial(per_device, mesh.shape["grp"], mesh.shape["rd"])
    return jax.shard_map(
        body, mesh=mesh, in_specs=in_specs, out_specs=out_specs, check_vma=False
    )
```

```python
import functools
import math

import jax
import jax.numpy as jnp
from jax import lax
from jax.experimental import pallas as pl
from jax.experimental.pallas import tpu as pltpu
from jax.sharding import PartitionSpec as P

MESH_ID = pl.DeviceIdType.MESH
CHUNK = 128
UNROLL = 24


def spread_kernel(
    dims, labels, degree, seeds, wanted, slots, tiles_hbm, out, *scratch
):
    groups, y_size, x_size, own, rows, near, chunks, cap = dims
    pool = scratch[:chunks]
    sent = scratch[chunks : 2 * chunks]
    landed = scratch[2 * chunks : 3 * chunks]
    weight, seed_class, tiles, tile_sem, x_send, x_recv, y_send, y_recv, s_send, s_recv, z_send, z_recv = scratch[
        3 * chunks :
    ]
    g = lax.axis_index("grp")
    me = lax.axis_index("rd")
    core = lax.rem(me, 2)
    x = lax.rem(lax.div(me, 2), x_size)
    y = lax.div(me, 2 * x_size)
    half = own // 2

    def device(yy, xx, cc):
        return (yy * x_size + xx) * 2 + cc

    def x_at(step):
        return lax.rem(x + step, x_size)

    def y_at(step):
        return lax.rem(y + step, y_size)

    sibling = device(y, x, 1 - core)

    tile_copies = []
    for d in range(groups):
        q = lax.rem(g + d, groups)
        copy = pltpu.make_async_copy(
            tiles_hbm.at[0, 0, q], tiles.at[pl.ds(q * near, near)], tile_sem.at[d]
        )
        tile_copies.append(copy)

    barrier = pltpu.get_barrier_semaphore()
    peers = [(g, device(y, x_at(i), core)) for i in range(1, x_size)]
    peers += [(g, device(y_at(i), x, core)) for i in range(1, y_size)]
    peers += [(g, sibling)]
    peers += [(lax.rem(g + d, groups), me) for d in range(1, groups)]
    for peer in peers:
        pl.semaphore_signal(barrier, inc=1, device_id=peer, device_id_type=MESH_ID)
    for copy in tile_copies:
        copy.start()

    lanes = 128
    eye = lax.broadcasted_iota(jnp.int32, (lanes, lanes), 0) == lax.broadcasted_iota(
        jnp.int32, (lanes, lanes), 1
    )

    def column_of(row):
        spread_row = jnp.broadcast_to(row, (lanes, lanes))
        return jnp.sum(jnp.where(eye, spread_row, 0.0), axis=1, keepdims=True)

    per_block = rows // lanes

    def scale(columns):
        def body(part, carry):
            factor = lax.rsqrt(column_of(degree[pl.ds(part, 1), :]))
            block = me * own + lax.div(part, per_block)
            first = lax.rem(part, per_block) * lanes
            for c in columns:
                piece = labels[pl.ds(part * lanes, lanes), c * CHUNK : (c + 1) * CHUNK]
                pool[c][block, pl.ds(first, lanes), :] = (
                    piece.astype(jnp.float32) * factor
                ).astype(jnp.bfloat16)
            return carry

        lax.fori_loop(0, own * per_block, body, 0)

    scale([0])
    pl.semaphore_wait(barrier, len(peers))

    pending = []

    def copy_of(c, first, count, send, recv, target):
        view = pool[c].at[pl.ds(first, count)]
        return pltpu.make_async_remote_copy(
            src_ref=view,
            dst_ref=view,
            send_sem=send,
            recv_sem=recv,
            device_id=target,
            device_id_type=MESH_ID,
        )

    def x_copy(c, i, j, which, source, target):
        return copy_of(
            c,
            source * own + which * half,
            half,
            x_send.at[c, i, j, which],
            x_recv.at[c, i, j, which],
            (g, target),
        )

    def y_copy(c, i, j, which, source, target):
        return copy_of(
            c,
            source * own + which * half,
            half,
            y_send.at[c, i, j, which],
            y_recv.at[c, i, j, which],
            (g, target),
        )

    def s_copy(c, i, j, source):
        return copy_of(
            c, source * own, own, s_send.at[c, i, j], s_recv.at[c, i, j], (g, sibling)
        )

    def start(copy):
        copy.start()
        pending.append(copy)

    def send_own(c, which):
        for j in range(1, x_size):
            start(x_copy(c, 0, j, which, me, device(y, x_at(j), core)))
        for i in range(1, y_size):
            start(y_copy(c, i, 0, 1 - which, me, device(y_at(i), x, core)))
        if which == 0:
            start(s_copy(c, 0, 0, me))

    def forward(c):
        for j in range(1, x_size):
            source = device(y, x_at(x_size - j), core)
            x_copy(c, 0, j, 0, source, sibling).wait_recv()
            for i in range(1, y_size):
                start(y_copy(c, i, j, 0, source, device(y_at(i), x, core)))
        for i in range(1, y_size):
            source = device(y_at(y_size - i), x, core)
            y_copy(c, i, 0, 1, source, sibling).wait_recv()
            for j in range(1, x_size):
                start(x_copy(c, i, j, 1, source, device(y, x_at(j), core)))

    def complete(c):
        for j in range(1, x_size):
            source = device(y, x_at(x_size - j), core)
            x_copy(c, 0, j, 1, source, sibling).wait_recv()
            start(s_copy(c, 0, j, source))
        for i in range(1, y_size):
            source = device(y_at(y_size - i), x, core)
            y_copy(c, i, 0, 0, source, sibling).wait_recv()
            start(s_copy(c, i, 0, source))
        for i in range(1, y_size):
            for j in range(1, x_size):
                source = device(y_at(y_size - i), x_at(x_size - j), core)
                y_copy(c, i, j, 0, source, sibling).wait_recv()
                x_copy(c, i, j, 1, source, sibling).wait_recv()
                start(s_copy(c, i, j, source))
        for i in range(y_size):
            for j in range(x_size):
                source = device(y_at(y_size - i), x_at(x_size - j), 1 - core)
                s_copy(c, i, j, source).wait_recv()

    def block_of(q, k):
        slot = slots[0, 0, q, k]
        source = lax.div(slot, cap)
        local = wanted[0, 0, lax.rem(slot, cap), source]
        return source * own + jnp.maximum(local, 0)

    def z_copy(c, d):
        return pltpu.make_async_remote_copy(
            src_ref=sent[c].at[d - 1],
            dst_ref=landed[c].at[d - 1],
            send_sem=z_send.at[c, d - 1],
            recv_sem=z_recv.at[c, d - 1],
            device_id=(lax.rem(g + d, groups), me),
            device_id_type=MESH_ID,
        )

    def compute(c):
        def piece(i, carry):
            d = lax.rem(i + 1, groups)
            q = lax.rem(g + d, groups)

            def body(step, acc):
                ks = [step * UNROLL + u for u in range(UNROLL)]
                left = jnp.concatenate([tiles[q * near + k] for k in ks], axis=1)
                right = jnp.concatenate([pool[c][block_of(q, k)] for k in ks], axis=0)
                return acc + jnp.dot(left, right, preferred_element_type=jnp.float32)

            acc = jnp.zeros((rows, CHUNK), jnp.float32)
            if near == UNROLL:
                acc = body(0, acc)
            else:
                acc = lax.fori_loop(0, near // UNROLL, body, acc)
            out[:, c * CHUNK : (c + 1) * CHUNK] = acc

            @pl.when(i < groups - 1)
            def _():
                sent[c][i] = acc.astype(jnp.bfloat16)
                z_copy(c, i + 1).start()

            return carry

        lax.fori_loop(0, groups, piece, 0)
        pending.extend(z_copy(c, d) for d in range(1, groups))

    def finish(c):
        total = out[:, c * CHUNK : (c + 1) * CHUNK]
        for d in range(1, groups):
            z_copy(c, d).wait_recv()
            total = total + landed[c][d - 1].astype(jnp.float32)
        classes = c * CHUNK + lax.broadcasted_iota(jnp.int32, (rows, CHUNK), 1)
        hit = jnp.where(seed_class[...] == classes, 1.0, 0.0)
        out[:, c * CHUNK : (c + 1) * CHUNK] = weight[...] * total + 0.2 * hit

    send_own(0, 0)
    send_own(0, 1)
    scale(range(1, chunks))
    if chunks > 1:
        send_own(1, 0)
    forward(0)
    for part in range(per_block):
        at = pl.ds(part * lanes, lanes)
        factor = 0.8 * lax.rsqrt(column_of(degree[pl.ds(part, 1), :]))
        weight[at, :] = jnp.broadcast_to(factor, (lanes, CHUNK))
        label = column_of(seeds[pl.ds(part, 1), :].astype(jnp.float32))
        seed_class[at, :] = jnp.broadcast_to(label, (lanes, CHUNK)).astype(jnp.int32)
    for c in range(chunks):
        if c + 1 < chunks:
            send_own(c + 1, 1)
        if c + 2 < chunks:
            send_own(c + 2, 0)
        if c + 1 < chunks:
            forward(c + 1)
        if c >= 2:
            finish(c - 2)
        complete(c)
        if c == 0:
            for copy in tile_copies:
                copy.wait()
        compute(c)
    for c in range(max(chunks - 2, 0), chunks):
        finish(c)
    for copy in pending:
        copy.wait_send()


def per_device(groups, readers, label_scores, degree, seed_label, wanted, nbr_slot, tiles):
    rows = tiles.shape[-1]
    classes = label_scores.shape[1]
    own = label_scores.shape[0] // rows
    near = nbr_slot.shape[-1]
    cap = wanted.shape[-1]
    chunks = classes // CHUNK
    chips = readers // 2
    x_size = math.isqrt(chips)
    y_size = chips // x_size
    dims = (groups, y_size, x_size, own, rows, near, chunks, cap)
    dma = pltpu.SemaphoreType.DMA
    vmem = pl.BlockSpec(memory_space=pltpu.VMEM)
    smem = pl.BlockSpec(memory_space=pltpu.SMEM)
    return pl.pallas_call(
        functools.partial(spread_kernel, dims),
        out_shape=jax.ShapeDtypeStruct((rows, classes), jnp.float32),
        in_specs=[vmem, vmem, vmem, smem, smem, pl.BlockSpec(memory_space=pl.ANY)],
        out_specs=vmem,
        scratch_shapes=[
            pltpu.VMEM((readers * own, rows, CHUNK), jnp.bfloat16) for _ in range(chunks)
        ]
        + [pltpu.VMEM((groups - 1, rows, CHUNK), jnp.bfloat16) for _ in range(2 * chunks)]
        + [
            pltpu.VMEM((rows, CHUNK), jnp.float32),
            pltpu.VMEM((rows, CHUNK), jnp.int32),
            pltpu.VMEM((groups * near, rows, rows), jnp.bfloat16),
            dma((groups,)),
            dma((chunks, y_size, x_size, 2)),
            dma((chunks, y_size, x_size, 2)),
            dma((chunks, y_size, x_size, 2)),
            dma((chunks, y_size, x_size, 2)),
            dma((chunks, y_size, x_size)),
            dma((chunks, y_size, x_size)),
            dma((chunks, groups - 1)),
            dma((chunks, groups - 1)),
        ],
        compiler_params=pltpu.CompilerParams(
            collective_id=0, has_side_effects=True, vmem_limit_bytes=60 * 1024 * 1024
        ),
    )(
        label_scores,
        degree.reshape(-1, 128),
        seed_label.reshape(-1, 128),
        jnp.swapaxes(wanted, 2, 3),
        nbr_slot,
        tiles,
    )


def solution(mesh):
    in_specs = (
        P(("grp", "rd"), None),
        P(("grp", "rd")),
        P(("grp", "rd")),
        P("grp", "rd", None, None),
        P("grp", "rd", None, None),
        P("grp", "rd", None, None, None, None),
    )
    out_specs = P(("grp", "rd"), None)
    body = functools.partial(per_device, mesh.shape["grp"], mesh.shape["rd"])
    return jax.shard_map(
        body, mesh=mesh, in_specs=in_specs, out_specs=out_specs, check_vma=False
    )
```

```python
import functools
import math

import jax
import jax.numpy as jnp
from jax import lax
from jax.experimental import pallas as pl
from jax.experimental.pallas import tpu as pltpu
from jax.sharding import PartitionSpec as P

MESH_ID = pl.DeviceIdType.MESH
CHUNK = 128
UNROLL = 24
SPLIT = 1


def spread_kernel(
    dims, labels, degree, seeds, wanted, slots, tiles_hbm, out, *scratch
):
    groups, y_size, x_size, own, rows, near, chunks, cap = dims
    pool = scratch[:chunks]
    sent = scratch[chunks : 2 * chunks]
    landed = scratch[2 * chunks : 3 * chunks]
    weight, seed_class, total_buf, label_buf, label_sem, out_sem, tiles, tile_sem, x_send, x_recv, y_send, y_recv, s_send, s_recv, z_send, z_recv = scratch[
        3 * chunks :
    ]
    g = lax.axis_index("grp")
    me = lax.axis_index("rd")
    core = lax.rem(me, 2)
    x = lax.rem(lax.div(me, 2), x_size)
    y = lax.div(me, 2 * x_size)
    half = own // 2

    def device(yy, xx, cc):
        return (yy * x_size + xx) * 2 + cc

    def x_at(step):
        return lax.rem(x + step, x_size)

    def y_at(step):
        return lax.rem(y + step, y_size)

    sibling = device(y, x, 1 - core)

    tile_copies = []
    for d in range(groups):
        q = lax.rem(g + d, groups)
        copy = pltpu.make_async_copy(
            tiles_hbm.at[0, 0, q], tiles.at[pl.ds(q * near, near)], tile_sem.at[d]
        )
        tile_copies.append(copy)

    barrier = pltpu.get_barrier_semaphore()
    peers = [(g, device(y, x_at(i), core)) for i in range(1, x_size)]
    peers += [(g, device(y_at(i), x, core)) for i in range(1, y_size)]
    peers += [(g, sibling)]
    peers += [(lax.rem(g + d, groups), me) for d in range(1, groups)]
    for peer in peers:
        pl.semaphore_signal(barrier, inc=1, device_id=peer, device_id_type=MESH_ID)
    label_copies = [
        pltpu.make_async_copy(
            labels.at[:, pl.ds(c * CHUNK, CHUNK)], label_buf.at[c], label_sem.at[c]
        )
        for c in range(chunks)
    ]
    for copy in label_copies + tile_copies:
        copy.start()

    lanes = 128
    eye = lax.broadcasted_iota(jnp.int32, (lanes, lanes), 0) == lax.broadcasted_iota(
        jnp.int32, (lanes, lanes), 1
    )

    def column_of(row):
        spread_row = jnp.broadcast_to(row, (lanes, lanes))
        return jnp.sum(jnp.where(eye, spread_row, 0.0), axis=1, keepdims=True)

    per_block = rows // lanes

    def scale(columns):
        for c in columns:
            label_copies[c].wait()

        def body(part, carry):
            factor = lax.rsqrt(column_of(degree[pl.ds(part, 1), :]))
            block = me * own + lax.div(part, per_block)
            first = lax.rem(part, per_block) * lanes
            for c in columns:
                piece = label_buf[c, pl.ds(part * lanes, lanes), :]
                pool[c][block, pl.ds(first, lanes), :] = (
                    piece.astype(jnp.float32) * factor
                ).astype(jnp.bfloat16)
            return carry

        lax.fori_loop(0, own * per_block, body, 0)

    scale([0])
    pl.semaphore_wait(barrier, len(peers))

    pending = []

    def copy_of(c, first, count, send, recv, target):
        view = pool[c].at[pl.ds(first, count)]
        return pltpu.make_async_remote_copy(
            src_ref=view,
            dst_ref=view,
            send_sem=send,
            recv_sem=recv,
            device_id=target,
            device_id_type=MESH_ID,
        )

    def x_copy(c, i, j, which, source, target):
        return copy_of(
            c,
            source * own + which * half,
            half,
            x_send.at[c, i, j, which],
            x_recv.at[c, i, j, which],
            (g, target),
        )

    def y_copy(c, i, j, which, source, target):
        return copy_of(
            c,
            source * own + which * half,
            half,
            y_send.at[c, i, j, which],
            y_recv.at[c, i, j, which],
            (g, target),
        )

    def s_copy(c, i, j, source):
        return copy_of(
            c, source * own, own, s_send.at[c, i, j], s_recv.at[c, i, j], (g, sibling)
        )

    def start(copy):
        copy.start()
        pending.append(copy)

    def send_own(c, which):
        for j in range(1, x_size):
            start(x_copy(c, 0, j, which, me, device(y, x_at(j), core)))
        for i in range(1, y_size):
            start(y_copy(c, i, 0, 1 - which, me, device(y_at(i), x, core)))
        if which == 0:
            start(s_copy(c, 0, 0, me))

    def forward(c):
        for j in range(1, x_size):
            source = device(y, x_at(x_size - j), core)
            x_copy(c, 0, j, 0, source, sibling).wait_recv()
            for i in range(1, y_size):
                start(y_copy(c, i, j, 0, source, device(y_at(i), x, core)))
        for i in range(1, y_size):
            source = device(y_at(y_size - i), x, core)
            y_copy(c, i, 0, 1, source, sibling).wait_recv()
            for j in range(1, x_size):
                start(x_copy(c, i, j, 1, source, device(y, x_at(j), core)))

    def complete(c):
        for j in range(1, x_size):
            source = device(y, x_at(x_size - j), core)
            x_copy(c, 0, j, 1, source, sibling).wait_recv()
            start(s_copy(c, 0, j, source))
        for i in range(1, y_size):
            source = device(y_at(y_size - i), x, core)
            y_copy(c, i, 0, 0, source, sibling).wait_recv()
            start(s_copy(c, i, 0, source))
        for i in range(1, y_size):
            for j in range(1, x_size):
                source = device(y_at(y_size - i), x_at(x_size - j), core)
                y_copy(c, i, j, 0, source, sibling).wait_recv()
                x_copy(c, i, j, 1, source, sibling).wait_recv()
                start(s_copy(c, i, j, source))
        for i in range(y_size):
            for j in range(x_size):
                source = device(y_at(y_size - i), x_at(x_size - j), 1 - core)
                s_copy(c, i, j, source).wait_recv()

    def block_of(q, k):
        slot = slots[0, 0, q, k]
        source = lax.div(slot, cap)
        local = wanted[0, 0, lax.rem(slot, cap), source]
        return source * own + jnp.maximum(local, 0)

    def z_copy(c, d):
        return pltpu.make_async_remote_copy(
            src_ref=sent[c].at[d - 1],
            dst_ref=landed[c].at[d - 1],
            send_sem=z_send.at[c, d - 1],
            recv_sem=z_recv.at[c, d - 1],
            device_id=(lax.rem(g + d, groups), me),
            device_id_type=MESH_ID,
        )

    def compute(c, low, high):
        def piece(i, carry):
            d = lax.rem(i + 1, groups)
            q = lax.rem(g + d, groups)

            def body(step, acc):
                ks = [step * UNROLL + u for u in range(UNROLL)]
                left = jnp.concatenate([tiles[q * near + k] for k in ks], axis=1)
                right = jnp.concatenate([pool[c][block_of(q, k)] for k in ks], axis=0)
                return acc + jnp.dot(left, right, preferred_element_type=jnp.float32)

            acc = jnp.zeros((rows, CHUNK), jnp.float32)
            if near == UNROLL:
                acc = body(0, acc)
            else:
                acc = lax.fori_loop(0, near // UNROLL, body, acc)
            total_buf[c] = acc

            @pl.when(i < groups - 1)
            def _():
                sent[c][i] = acc.astype(jnp.bfloat16)
                z_copy(c, i + 1).start()

            return carry

        lax.fori_loop(low, high, piece, 0)

    out_copies = [
        pltpu.make_async_copy(
            total_buf.at[c], out.at[:, pl.ds(c * CHUNK, CHUNK)], out_sem.at[c]
        )
        for c in range(chunks)
    ]

    def finish(c):
        total = total_buf[c]
        for d in range(1, groups):
            z_copy(c, d).wait_recv()
            total = total + landed[c][d - 1].astype(jnp.float32)
        classes = c * CHUNK + lax.broadcasted_iota(jnp.int32, (rows, CHUNK), 1)
        hit = jnp.where(seed_class[...] == classes, 1.0, 0.0)
        total_buf[c] = weight[...] * total + 0.2 * hit
        out_copies[c].start()

    send_own(0, 0)
    send_own(0, 1)
    scale(range(1, chunks))
    forward(0)
    if chunks > 1:
        send_own(1, 0)
        send_own(1, 1)
    for part in range(per_block):
        at = pl.ds(part * lanes, lanes)
        factor = 0.8 * lax.rsqrt(column_of(degree[pl.ds(part, 1), :]))
        weight[at, :] = jnp.broadcast_to(factor, (lanes, CHUNK))
        label = column_of(seeds[pl.ds(part, 1), :].astype(jnp.float32))
        seed_class[at, :] = jnp.broadcast_to(label, (lanes, CHUNK)).astype(jnp.int32)
    for c in range(chunks):
        complete(c)
        if c == 0:
            for copy in tile_copies:
                copy.wait()
        if c + 1 < chunks:
            compute(c, 0, SPLIT)
            forward(c + 1)
            if c + 2 < chunks:
                send_own(c + 2, 0)
                send_own(c + 2, 1)
            compute(c, SPLIT, groups)
            if c >= 1:
                finish(c - 1)
        else:
            compute(c, 0, groups)
        pending.extend(z_copy(c, d) for d in range(1, groups))
    for c in range(max(chunks - 2, 0), chunks):
        finish(c)
    for copy in pending:
        copy.wait_send()
    for copy in out_copies:
        copy.wait()


def per_device(groups, readers, label_scores, degree, seed_label, wanted, nbr_slot, tiles):
    rows = tiles.shape[-1]
    classes = label_scores.shape[1]
    own = label_scores.shape[0] // rows
    near = nbr_slot.shape[-1]
    cap = wanted.shape[-1]
    chunks = classes // CHUNK
    chips = readers // 2
    x_size = math.isqrt(chips)
    y_size = chips // x_size
    dims = (groups, y_size, x_size, own, rows, near, chunks, cap)
    dma = pltpu.SemaphoreType.DMA
    vmem = pl.BlockSpec(memory_space=pltpu.VMEM)
    smem = pl.BlockSpec(memory_space=pltpu.SMEM)
    return pl.pallas_call(
        functools.partial(spread_kernel, dims),
        out_shape=jax.ShapeDtypeStruct((rows, classes), jnp.float32),
        in_specs=[pl.BlockSpec(memory_space=pl.ANY), vmem, vmem, smem, smem, pl.BlockSpec(memory_space=pl.ANY)],
        out_specs=pl.BlockSpec(memory_space=pl.ANY),
        scratch_shapes=[
            pltpu.VMEM((readers * own, rows, CHUNK), jnp.bfloat16) for _ in range(chunks)
        ]
        + [pltpu.VMEM((groups - 1, rows, CHUNK), jnp.bfloat16) for _ in range(2 * chunks)]
        + [
            pltpu.VMEM((rows, CHUNK), jnp.float32),
            pltpu.VMEM((rows, CHUNK), jnp.int32),
            pltpu.VMEM((chunks, rows, CHUNK), jnp.float32),
            pltpu.VMEM((chunks, own * rows, CHUNK), jnp.bfloat16),
            dma((chunks,)),
            dma((chunks,)),
            pltpu.VMEM((groups * near, rows, rows), jnp.bfloat16),
            dma((groups,)),
            dma((chunks, y_size, x_size, 2)),
            dma((chunks, y_size, x_size, 2)),
            dma((chunks, y_size, x_size, 2)),
            dma((chunks, y_size, x_size, 2)),
            dma((chunks, y_size, x_size)),
            dma((chunks, y_size, x_size)),
            dma((chunks, groups - 1)),
            dma((chunks, groups - 1)),
        ],
        compiler_params=pltpu.CompilerParams(
            collective_id=0, has_side_effects=True, vmem_limit_bytes=60 * 1024 * 1024
        ),
    )(
        label_scores,
        degree.reshape(-1, 128),
        seed_label.reshape(-1, 128),
        jnp.swapaxes(wanted, 2, 3),
        nbr_slot,
        tiles,
    )


def solution(mesh):
    in_specs = (
        P(("grp", "rd"), None),
        P(("grp", "rd")),
        P(("grp", "rd")),
        P("grp", "rd", None, None),
        P("grp", "rd", None, None),
        P("grp", "rd", None, None, None, None),
    )
    out_specs = P(("grp", "rd"), None)
    body = functools.partial(per_device, mesh.shape["grp"], mesh.shape["rd"])
    return jax.shard_map(
        body, mesh=mesh, in_specs=in_specs, out_specs=out_specs, check_vma=False
    )
```

```python
import functools
import math

import jax
import jax.numpy as jnp
from jax import lax
from jax.experimental import pallas as pl
from jax.experimental.pallas import tpu as pltpu
from jax.sharding import PartitionSpec as P

MESH_ID = pl.DeviceIdType.MESH
CHUNK = 128
UNROLL = 24
SPLIT = 0


def spread_kernel(
    dims, labels, degree, seeds, wanted, slots, tiles_hbm, out, *scratch
):
    groups, y_size, x_size, own, rows, near, chunks, cap = dims
    pool = scratch[:chunks]
    sent = scratch[chunks : 2 * chunks]
    landed = scratch[2 * chunks : 3 * chunks]
    weight, seed_class, total_buf, label_buf, label_sem, out_sem, tiles, tile_sem, x_send, x_recv, y_send, y_recv, s_send, s_recv, z_send, z_recv = scratch[
        3 * chunks :
    ]
    g = lax.axis_index("grp")
    me = lax.axis_index("rd")
    core = lax.rem(me, 2)
    x = lax.rem(lax.div(me, 2), x_size)
    y = lax.div(me, 2 * x_size)
    half = own // 2

    def device(yy, xx, cc):
        return (yy * x_size + xx) * 2 + cc

    def x_at(step):
        return lax.rem(x + step, x_size)

    def y_at(step):
        return lax.rem(y + step, y_size)

    sibling = device(y, x, 1 - core)

    tile_copies = []
    for d in range(groups):
        q = lax.rem(g + d, groups)
        copy = pltpu.make_async_copy(
            tiles_hbm.at[0, 0, q], tiles.at[pl.ds(q * near, near)], tile_sem.at[d]
        )
        tile_copies.append(copy)

    barrier = pltpu.get_barrier_semaphore()
    peers = [(g, device(y, x_at(i), core)) for i in range(1, x_size)]
    peers += [(g, device(y_at(i), x, core)) for i in range(1, y_size)]
    peers += [(g, sibling)]
    peers += [(lax.rem(g + d, groups), me) for d in range(1, groups)]
    for peer in peers:
        pl.semaphore_signal(barrier, inc=1, device_id=peer, device_id_type=MESH_ID)
    label_copies = [
        pltpu.make_async_copy(
            labels.at[:, pl.ds(c * CHUNK, CHUNK)], label_buf.at[c], label_sem.at[c]
        )
        for c in range(chunks)
    ]
    for copy in label_copies + tile_copies:
        copy.start()

    lanes = 128
    eye = lax.broadcasted_iota(jnp.int32, (lanes, lanes), 0) == lax.broadcasted_iota(
        jnp.int32, (lanes, lanes), 1
    )

    def column_of(row):
        spread_row = jnp.broadcast_to(row, (lanes, lanes))
        return jnp.sum(jnp.where(eye, spread_row, 0.0), axis=1, keepdims=True)

    per_block = rows // lanes

    def scale(columns):
        for c in columns:
            label_copies[c].wait()

        def body(part, carry):
            factor = lax.rsqrt(column_of(degree[pl.ds(part, 1), :]))
            block = me * own + lax.div(part, per_block)
            first = lax.rem(part, per_block) * lanes
            for c in columns:
                piece = label_buf[c, pl.ds(part * lanes, lanes), :]
                pool[c][block, pl.ds(first, lanes), :] = (
                    piece.astype(jnp.float32) * factor
                ).astype(jnp.bfloat16)
            return carry

        lax.fori_loop(0, own * per_block, body, 0)

    scale([0])
    pl.semaphore_wait(barrier, len(peers))

    pending = []

    def copy_of(c, first, count, send, recv, target):
        view = pool[c].at[pl.ds(first, count)]
        return pltpu.make_async_remote_copy(
            src_ref=view,
            dst_ref=view,
            send_sem=send,
            recv_sem=recv,
            device_id=target,
            device_id_type=MESH_ID,
        )

    def x_copy(c, i, j, which, source, target):
        return copy_of(
            c,
            source * own + which * half,
            half,
            x_send.at[c, i, j, which],
            x_recv.at[c, i, j, which],
            (g, target),
        )

    def y_copy(c, i, j, which, source, target):
        return copy_of(
            c,
            source * own + which * half,
            half,
            y_send.at[c, i, j, which],
            y_recv.at[c, i, j, which],
            (g, target),
        )

    def s_copy(c, i, j, source):
        return copy_of(
            c, source * own, own, s_send.at[c, i, j], s_recv.at[c, i, j], (g, sibling)
        )

    def start(copy):
        copy.start()
        pending.append(copy)

    def send_own(c, which):
        for j in range(1, x_size):
            start(x_copy(c, 0, j, which, me, device(y, x_at(j), core)))
        for i in range(1, y_size):
            start(y_copy(c, i, 0, 1 - which, me, device(y_at(i), x, core)))
        if which == 0:
            start(s_copy(c, 0, 0, me))

    def forward(c):
        for j in range(1, x_size):
            source = device(y, x_at(x_size - j), core)
            x_copy(c, 0, j, 0, source, sibling).wait_recv()
            for i in range(1, y_size):
                start(y_copy(c, i, j, 0, source, device(y_at(i), x, core)))
        for i in range(1, y_size):
            source = device(y_at(y_size - i), x, core)
            y_copy(c, i, 0, 1, source, sibling).wait_recv()
            for j in range(1, x_size):
                start(x_copy(c, i, j, 1, source, device(y, x_at(j), core)))

    def complete(c):
        for j in range(1, x_size):
            source = device(y, x_at(x_size - j), core)
            x_copy(c, 0, j, 1, source, sibling).wait_recv()
            start(s_copy(c, 0, j, source))
        for i in range(1, y_size):
            source = device(y_at(y_size - i), x, core)
            y_copy(c, i, 0, 0, source, sibling).wait_recv()
            start(s_copy(c, i, 0, source))
        for i in range(1, y_size):
            for j in range(1, x_size):
                source = device(y_at(y_size - i), x_at(x_size - j), core)
                y_copy(c, i, j, 0, source, sibling).wait_recv()
                x_copy(c, i, j, 1, source, sibling).wait_recv()
                start(s_copy(c, i, j, source))
        for i in range(y_size):
            for j in range(x_size):
                source = device(y_at(y_size - i), x_at(x_size - j), 1 - core)
                s_copy(c, i, j, source).wait_recv()

    def block_of(q, k):
        slot = slots[0, 0, q, k]
        source = lax.div(slot, cap)
        local = wanted[0, 0, lax.rem(slot, cap), source]
        return source * own + jnp.maximum(local, 0)

    def z_copy(c, d):
        return pltpu.make_async_remote_copy(
            src_ref=sent[c].at[d - 1],
            dst_ref=landed[c].at[d - 1],
            send_sem=z_send.at[c, d - 1],
            recv_sem=z_recv.at[c, d - 1],
            device_id=(lax.rem(g + d, groups), me),
            device_id_type=MESH_ID,
        )

    def compute(c, low, high):
        def piece(i, carry):
            d = lax.rem(i + 1, groups)
            q = lax.rem(g + d, groups)

            def body(step, acc):
                ks = [step * UNROLL + u for u in range(UNROLL)]
                left = jnp.concatenate([tiles[q * near + k] for k in ks], axis=1)
                right = jnp.concatenate([pool[c][block_of(q, k)] for k in ks], axis=0)
                return acc + jnp.dot(left, right, preferred_element_type=jnp.float32)

            acc = jnp.zeros((rows, CHUNK), jnp.float32)
            if near == UNROLL:
                acc = body(0, acc)
            else:
                acc = lax.fori_loop(0, near // UNROLL, body, acc)
            total_buf[c] = acc

            @pl.when(i < groups - 1)
            def _():
                sent[c][i] = acc.astype(jnp.bfloat16)
                z_copy(c, i + 1).start()

            return carry

        lax.fori_loop(low, high, piece, 0)

    out_copies = [
        pltpu.make_async_copy(
            total_buf.at[c], out.at[:, pl.ds(c * CHUNK, CHUNK)], out_sem.at[c]
        )
        for c in range(chunks)
    ]

    def finish(c):
        total = total_buf[c]
        for d in range(1, groups):
            z_copy(c, d).wait_recv()
            total = total + landed[c][d - 1].astype(jnp.float32)
        classes = c * CHUNK + lax.broadcasted_iota(jnp.int32, (rows, CHUNK), 1)
        hit = jnp.where(seed_class[...] == classes, 1.0, 0.0)
        total_buf[c] = weight[...] * total + 0.2 * hit
        out_copies[c].start()

    send_own(0, 0)
    send_own(0, 1)
    scale(range(1, chunks))
    forward(0)
    if chunks > 1:
        send_own(1, 0)
        send_own(1, 1)
    for part in range(per_block):
        at = pl.ds(part * lanes, lanes)
        factor = 0.8 * lax.rsqrt(column_of(degree[pl.ds(part, 1), :]))
        weight[at, :] = jnp.broadcast_to(factor, (lanes, CHUNK))
        label = column_of(seeds[pl.ds(part, 1), :].astype(jnp.float32))
        seed_class[at, :] = jnp.broadcast_to(label, (lanes, CHUNK)).astype(jnp.int32)
    for c in range(chunks):
        complete(c)
        if c == 0:
            for copy in tile_copies:
                copy.wait()
        if c + 1 < chunks:
            compute(c, 0, SPLIT)
            forward(c + 1)
            if c + 2 < chunks:
                send_own(c + 2, 0)
                send_own(c + 2, 1)
            compute(c, SPLIT, groups)
            if c >= 1:
                finish(c - 1)
        else:
            compute(c, 0, groups)
        pending.extend(z_copy(c, d) for d in range(1, groups))
    for c in range(max(chunks - 2, 0), chunks):
        finish(c)
    for copy in pending:
        copy.wait_send()
    for copy in out_copies:
        copy.wait()


def per_device(groups, readers, label_scores, degree, seed_label, wanted, nbr_slot, tiles):
    rows = tiles.shape[-1]
    classes = label_scores.shape[1]
    own = label_scores.shape[0] // rows
    near = nbr_slot.shape[-1]
    cap = wanted.shape[-1]
    chunks = classes // CHUNK
    chips = readers // 2
    x_size = math.isqrt(chips)
    y_size = chips // x_size
    dims = (groups, y_size, x_size, own, rows, near, chunks, cap)
    dma = pltpu.SemaphoreType.DMA
    vmem = pl.BlockSpec(memory_space=pltpu.VMEM)
    smem = pl.BlockSpec(memory_space=pltpu.SMEM)
    return pl.pallas_call(
        functools.partial(spread_kernel, dims),
        out_shape=jax.ShapeDtypeStruct((rows, classes), jnp.float32),
        in_specs=[pl.BlockSpec(memory_space=pl.ANY), vmem, vmem, smem, smem, pl.BlockSpec(memory_space=pl.ANY)],
        out_specs=pl.BlockSpec(memory_space=pl.ANY),
        scratch_shapes=[
            pltpu.VMEM((readers * own, rows, CHUNK), jnp.bfloat16) for _ in range(chunks)
        ]
        + [pltpu.VMEM((groups - 1, rows, CHUNK), jnp.bfloat16) for _ in range(2 * chunks)]
        + [
            pltpu.VMEM((rows, CHUNK), jnp.float32),
            pltpu.VMEM((rows, CHUNK), jnp.int32),
            pltpu.VMEM((chunks, rows, CHUNK), jnp.float32),
            pltpu.VMEM((chunks, own * rows, CHUNK), jnp.bfloat16),
            dma((chunks,)),
            dma((chunks,)),
            pltpu.VMEM((groups * near, rows, rows), jnp.bfloat16),
            dma((groups,)),
            dma((chunks, y_size, x_size, 2)),
            dma((chunks, y_size, x_size, 2)),
            dma((chunks, y_size, x_size, 2)),
            dma((chunks, y_size, x_size, 2)),
            dma((chunks, y_size, x_size)),
            dma((chunks, y_size, x_size)),
            dma((chunks, groups - 1)),
            dma((chunks, groups - 1)),
        ],
        compiler_params=pltpu.CompilerParams(
            collective_id=0, has_side_effects=True, vmem_limit_bytes=60 * 1024 * 1024
        ),
    )(
        label_scores,
        degree.reshape(-1, 128),
        seed_label.reshape(-1, 128),
        jnp.swapaxes(wanted, 2, 3),
        nbr_slot,
        tiles,
    )


def solution(mesh):
    in_specs = (
        P(("grp", "rd"), None),
        P(("grp", "rd")),
        P(("grp", "rd")),
        P("grp", "rd", None, None),
        P("grp", "rd", None, None),
        P("grp", "rd", None, None, None, None),
    )
    out_specs = P(("grp", "rd"), None)
    body = functools.partial(per_device, mesh.shape["grp"], mesh.shape["rd"])
    return jax.shard_map(
        body, mesh=mesh, in_specs=in_specs, out_specs=out_specs, check_vma=False
    )
```
